768 devices in a mesh: rep: 12 (over z), shard: 64 (over x, y, core).
Axes of the slice: x: 4, y: 8, z: 12, core: 2. Of those that a mesh axis runs over, the one named last changes fastest.
Arguments:
- grad_parts: bfloat16 [12, 96, 256, 3584], P('rep', None, 'shard'), may hold values from -6 to 6
- momentum: float32 [96, 256, 3584], P('rep', 'shard'), may hold values from -131 to 131
- mask_codes: int32 [96, 256, 896], P('rep', 'shard'), may hold values from 0 to 5
Outputs:
- momentum_next: float32 [96, 256, 3584], P('rep', 'shard')
- update: bfloat16 [96, 256, 3584], P('rep', 'shard')
The draws below stay inside these ranges and needn't reach their ends.
Inputs may be any that keep to these rules, and one draw needn't show every extreme that they name: `mask_codes`: code k names the kept pair of columns of a group of four as in the reference program.
All inputs are finite; a program needn't handle non-finite values.
Results may differ from the reference program's by a relative error of at most 0.02.
Values may be sent and summed in bfloat16 or wider, within the bound.
No kernel may reach another device: no remote copies, remote signals or barrier semaphores. Data moves between devices by JAX's collectives and lax.ppermute only.
A program may use at most 64 MiB of HBM per device.

```python
import math
import jax
import jax.numpy as jnp
from jax import lax

ROWS = 256
COLS = 3584
ITERS = 5
MATS = 96
N_REP = 12


def draw_momentum(key, part):
    key = jax.random.fold_in(key, 7)
    key_base, key_rows, key_cols = jax.random.split(key, 3)
    spread = math.log(10.0)
    base = jnp.clip(jax.random.normal(key_base, (MATS, ROWS, COLS), jnp.float32), -4.0, 4.0)
    row_scale = jnp.exp(jax.random.uniform(key_rows, (MATS, ROWS, 1), jnp.float32, 0.0, spread))
    col_scale = jnp.exp(jax.random.uniform(key_cols, (MATS, 1, COLS), jnp.float32, 0.0, spread))
    return 0.3 * base * row_scale * col_scale


def set_ends(drawn, stream_key, smallest, high):
    shape = drawn.shape
    spot = [jax.random.randint(jax.random.fold_in(stream_key, axis), (), 0, shape[axis]) for axis in range(len(shape))]
    drawn = drawn.at[tuple(spot)].set(smallest)
    longest = shape.index(max(shape))
    spot[longest] = (spot[longest] + 1) % shape[longest]
    return drawn.at[tuple(spot)].set(high)


def with_spikes(values, rng, source, target, shards_of, factor):
    def block_of(axis_at):
        return (jnp.arange(values.shape[axis_at]) // (values.shape[axis_at] // shards_of)).reshape((-1,) + (1,) * (values.ndim - 1 - axis_at))

    one_side = jax.random.permutation(rng, shards_of)[block_of(target)]
    other_side = (block_of(target) + shards_of // 2) % shards_of
    return jnp.where((block_of(source) == one_side) | (block_of(source) == other_side), factor * values, values)


def level_of(stream_key, extent, pieces, smallest, high):
    factor_of, own = 1.0, jax.random.fold_in(stream_key, 6)
    for dim, blocks in pieces:
        heights = jnp.exp(jax.random.uniform(jax.random.fold_in(own, dim), (blocks,), jnp.float32, smallest / len(pieces), high / len(pieces)))
        factor_of = factor_of * jnp.repeat(heights, extent[dim] // blocks).reshape([-1 if axis == dim else 1 for axis in range(len(extent))])
    return factor_of


def bell_draw_with(own_key, shape, scale, most, pieces, heavy, kind=jnp.bfloat16):
    array = scale * jax.random.normal(own_key, shape, jnp.float32)
    if pieces:
        array = array * level_of(own_key, shape, pieces, -0.22, 0.18)
    return jnp.clip(with_spikes(array, jax.random.fold_in(own_key, 3), *heavy), -most, most).astype(kind)


def setup_inputs(seed: int = 0) -> dict:
    streams_of = jax.random.split(jax.random.key(seed), 4)
    grad_parts = bell_draw_with(streams_of[0], (N_REP, MATS, ROWS, COLS), 1.0, 6.0, ((0, 12), (2, 64)), (0, 1, 12, 2.0))
    momentum = draw_momentum(jax.random.fold_in(streams_of[3], 71), 0)
    mask_codes = set_ends(jax.random.randint(streams_of[2], (MATS, ROWS, COLS // 4), 0, 6), jax.random.fold_in(streams_of[2], 1), 0, 5).astype(jnp.int32)
    return {"grad_parts": grad_parts, "momentum": momentum, "mask_codes": mask_codes}


DECAY_RATE = 0.95
EPSILON = 1e-07
QUINTIC_FIRST = 3.4445
QUINTIC_SECOND = -4.775
QUINTIC_THIRD = 2.0315
UPDATE_SCALE = 64.0

def keep_columns(code_array):
    holders = ((0, 1, 2), (0, 3, 4), (1, 3, 5), (2, 4, 5))
    parts = []
    for codes_here in holders:
        hit = (code_array == codes_here[0]) | (code_array == codes_here[1]) | (code_array == codes_here[2])
        parts.append(hit.astype(jnp.float32))
    stacked = jnp.stack(parts, axis=-1)
    return stacked.reshape(code_array.shape[:-1] + (code_array.shape[-1] * 4,))

def coefficients(gram_matrix):
    row_total = gram_matrix.shape[0]
    trace_sum = jnp.trace(gram_matrix)
    inverse = lax.rsqrt(trace_sum + EPSILON)
    scaled = gram_matrix * (inverse * inverse)
    identity = jnp.eye(row_total, dtype=jnp.float32)
    factor_now = identity
    for iteration in range(ITERS):
        product = jnp.dot(factor_now, scaled, precision=lax.Precision.HIGHEST)
        square_form = jnp.dot(product, factor_now.T, precision=lax.Precision.HIGHEST)
        polynomial = QUINTIC_FIRST * identity + QUINTIC_SECOND * square_form + QUINTIC_THIRD * jnp.dot(square_form, square_form, precision=lax.Precision.HIGHEST)
        factor_now = jnp.dot(polynomial, factor_now, precision=lax.Precision.HIGHEST)
    return (factor_now * inverse).astype(jnp.bfloat16)

def orthogonalize(inputs_bf):
    gram_matrix = lax.dot_general(inputs_bf, inputs_bf, (((1,), (1,)), ((), ())), preferred_element_type=jnp.float32)
    coef = coefficients(gram_matrix)
    return jnp.dot(coef, inputs_bf, preferred_element_type=jnp.float32).astype(jnp.bfloat16)

def reference(grad_parts, momentum, mask_codes):
    accumulated = jnp.zeros(momentum.shape, jnp.float32)
    for replica in range(N_REP):
        accumulated = accumulated + grad_parts[replica].astype(jnp.float32)
    momentum_next = DECAY_RATE * momentum + accumulated
    inputs_bf = momentum_next.astype(jnp.bfloat16)

    def one_matrix(pair):
        matrix_bf, code_array = pair
        orthogonal = orthogonalize(matrix_bf)
        kept_mask = keep_columns(code_array)
        return (UPDATE_SCALE * kept_mask * orthogonal.astype(jnp.float32)).astype(jnp.bfloat16)
    update = lax.map(one_matrix, (inputs_bf, mask_codes))
    return (momentum_next, update)
```

```python
import jax
import jax.numpy as jnp
from jax import lax
from jax.experimental import pallas as pl
from jax.experimental.pallas import tpu as pltpu
from jax.sharding import PartitionSpec as P

ITERS = 5
DECAY_RATE = 0.95
EPSILON = 1e-07
QUINTIC_FIRST = 3.4445
QUINTIC_SECOND = -4.775
QUINTIC_THIRD = 2.0315
UPDATE_SCALE = 64.0

REPS = 12
MATS_HERE = 8
PIECE_ROWS = 4
COLS = 3584
SHARDS = 64
ROWS = 256
SLICE = 512
SLICES_USED = COLS // SLICE
HALF = ROWS // 2
BF = jnp.bfloat16
F32 = jnp.float32
PARAMS = pltpu.CompilerParams(vmem_limit_bytes=40 * 1024 * 1024)
GROUP_BITS = (1, 2, 16)


def device_of(matrix, column_slice):
    return (
        (matrix >> 2) * 32
        + (column_slice >> 2) * 16
        + (matrix & 3) * 4
        + (column_slice & 3)
    )


def vmem():
    return pl.BlockSpec(memory_space=pltpu.VMEM)


def mask_kernel(codes_ref, mask_ref):
    group = lax.broadcasted_iota(jnp.int32, (128, 512), 0)
    column = lax.broadcasted_iota(jnp.int32, (128, 512), 1)
    spread = jnp.where((column >> 2) == group, 1.0, 0.0).astype(BF)
    place = lax.broadcasted_iota(jnp.int32, (32, 512), 1) & 3
    for block in range(7):
        code = codes_ref[:, block * 128 : (block + 1) * 128]
        pair = jnp.where(code == 0, 3, jnp.where(code == 1, 5, jnp.where(code == 2, 9, 0)))
        pair = jnp.where(code == 3, 6, jnp.where(code == 4, 10, jnp.where(code == 5, 12, pair)))
        wide = jnp.dot(pair.astype(F32).astype(BF), spread, preferred_element_type=F32).astype(jnp.int32)
        kept = ((wide >> place) & 1).astype(F32) * UPDATE_SCALE
        mask_ref[:, block * 512 : (block + 1) * 512] = kept.astype(BF)


def momentum_kernel(sum_ref, momentum_ref, next_ref, out_ref):
    for matrix in range(MATS_HERE):
        for column_slice in range(8):
            target = device_of(matrix, column_slice)
            if column_slice < SLICES_USED:
                here = slice(column_slice * SLICE, (column_slice + 1) * SLICE)
                value = DECAY_RATE * momentum_ref[matrix, :, here] + sum_ref[matrix, :, here].astype(F32)
                next_ref[matrix, :, here] = value
                out_ref[target] = value.astype(BF)
            else:
                out_ref[target] = jnp.zeros((PIECE_ROWS, SLICE), BF)


def gram_kernel(x_ref, packed_ref):
    def product(a, b):
        return lax.dot_general(a, b, (((1,), (1,)), ((), ())), preferred_element_type=F32)

    low = x_ref[:HALF, :]
    high = x_ref[HALF:, :]
    packed_ref[0] = product(low, low)
    packed_ref[1] = product(low, high)
    packed_ref[2] = product(high, high)


def orthogonal_kernel(packed_ref, x_ref, out_ref):
    def product(a, b):
        return jnp.dot(a, b, precision=lax.Precision.HIGHEST, preferred_element_type=F32)

    cross = packed_ref[1]
    gram = jnp.concatenate(
        [
            jnp.concatenate([packed_ref[0], cross], axis=1),
            jnp.concatenate([cross.T, packed_ref[2]], axis=1),
        ],
        axis=0,
    )
    diagonal = lax.broadcasted_iota(jnp.int32, (ROWS, ROWS), 0) == lax.broadcasted_iota(jnp.int32, (ROWS, ROWS), 1)
    trace_sum = jnp.sum(jnp.where(diagonal, gram, 0.0))
    inverse = lax.rsqrt(jnp.full((1, 1), trace_sum + EPSILON, F32))
    scaled = gram * (inverse * inverse)
    square_form = scaled
    factor = None
    for iteration in range(ITERS):
        polynomial = (
            jnp.where(diagonal, QUINTIC_FIRST, 0.0)
            + QUINTIC_SECOND * square_form
            + QUINTIC_THIRD * product(square_form, square_form)
        )
        factor = polynomial if factor is None else product(polynomial, factor)
        if iteration + 1 < ITERS:
            square_form = product(product(factor, scaled), factor.T)
    coef = (factor * inverse).astype(BF)
    out_ref[...] = jnp.dot(coef, x_ref[...], preferred_element_type=F32).astype(BF)


def update_kernel(returned_ref, mask_ref, update_ref):
    for matrix in range(MATS_HERE):
        for column_slice in range(SLICES_USED):
            here = slice(column_slice * SLICE, (column_slice + 1) * SLICE)
            value = returned_ref[device_of(matrix, column_slice)].astype(F32)
            update_ref[matrix, :, here] = (value * mask_ref[matrix, :, here].astype(F32)).astype(BF)


def call(kernel, outs, *args):
    return pl.pallas_call(
        kernel,
        out_shape=outs,
        in_specs=[vmem() for _ in args],
        out_specs=jax.tree.map(lambda _: vmem(), outs),
        compiler_params=PARAMS,
    )(*args)


def shaped(shape, dtype):
    return jax.ShapeDtypeStruct(shape, dtype)


def local(grad_parts, momentum, mask_codes):
    summed = lax.psum_scatter(
        grad_parts[0].reshape(REPS * MATS_HERE, PIECE_ROWS * COLS), "rep", scatter_dimension=0, tiled=True
    ).reshape(MATS_HERE, PIECE_ROWS, COLS)
    mask = call(mask_kernel, shaped((32, COLS), BF), mask_codes.reshape(32, COLS // 4))
    mask = mask.reshape(MATS_HERE, PIECE_ROWS, COLS)
    summed, mask = lax.optimization_barrier((summed, mask))
    momentum_next, outgoing = call(
        momentum_kernel,
        (shaped((MATS_HERE, PIECE_ROWS, COLS), F32), shaped((SHARDS, PIECE_ROWS, SLICE), BF)),
        summed,
        momentum,
    )
    gathered = lax.all_to_all(outgoing, "shard", split_axis=0, concat_axis=0, tiled=True)
    xmat = gathered.reshape(ROWS, SLICE)
    packed = call(gram_kernel, shaped((3, HALF, HALF), F32), xmat)
    for bit in GROUP_BITS:
        packed = packed + lax.ppermute(packed, "shard", [(i, i ^ bit) for i in range(SHARDS)])
    orthogonal = call(orthogonal_kernel, shaped((ROWS, SLICE), BF), packed, xmat)
    returned = lax.all_to_all(
        orthogonal.reshape(SHARDS, PIECE_ROWS, SLICE), "shard", split_axis=0, concat_axis=0, tiled=True
    )
    update = call(update_kernel, shaped((MATS_HERE, PIECE_ROWS, COLS), BF), returned, mask)
    return (momentum_next, update)


def solution(mesh):
    in_specs = (P("rep", None, "shard", None), P("rep", "shard", None), P("rep", "shard", None))
    out_specs = (P("rep", "shard", None), P("rep", "shard", None))
    return jax.shard_map(local, mesh=mesh, in_specs=in_specs, out_specs=out_specs, check_vma=False)
```

```python
import jax
import jax.numpy as jnp
from jax import lax
from jax.experimental import pallas as pl
from jax.experimental.pallas import tpu as pltpu
from jax.sharding import PartitionSpec as P

ITERS = 5
DECAY_RATE = 0.95
EPSILON = 1e-07
QUINTIC_FIRST = 3.4445
QUINTIC_SECOND = -4.775
QUINTIC_THIRD = 2.0315
UPDATE_SCALE = 64.0

MATS_HERE = 8
PIECE_ROWS = 4
COLS = 3584
ROWS = 256
HALF = ROWS // 2
PLANE_X = 4
PLANE_Y = 8
CORES = 2
SHARDS = PLANE_X * PLANE_Y * CORES
OWN_ROWS = PLANE_Y * PIECE_ROWS
BF = jnp.bfloat16
F32 = jnp.float32
CHUNK = (MATS_HERE, PIECE_ROWS, COLS)
PARAMS = pltpu.CompilerParams(vmem_limit_bytes=24 * 1024 * 1024)
NT = (((1,), (1,)), ((), ()))


def shard_index(x, y, core):
    return (x * PLANE_Y + y) * CORES + core


GROUPS_Y = [[shard_index(x, y, c) for y in range(PLANE_Y)] for x in range(PLANE_X) for c in range(CORES)]
GROUPS_X = [[shard_index(x, y, c) for x in range(PLANE_X)] for y in range(PLANE_Y) for c in range(CORES)]
OTHER_CORE = [(i, i ^ 1) for i in range(SHARDS)]


def vmem():
    return pl.BlockSpec(memory_space=pltpu.VMEM)


def smem():
    return pl.BlockSpec(memory_space=pltpu.SMEM)


def mask_kernel(codes_ref, mask_ref):
    group = lax.broadcasted_iota(jnp.int32, (128, 512), 0)
    column = lax.broadcasted_iota(jnp.int32, (128, 512), 1)
    spread = jnp.where((column >> 2) == group, 1.0, 0.0).astype(BF)
    place = lax.broadcasted_iota(jnp.int32, (32, 512), 1) & 3
    for block in range(7):
        code = codes_ref[:, block * 128 : (block + 1) * 128]
        pair = jnp.where(code == 0, 3, jnp.where(code == 1, 5, jnp.where(code == 2, 9, 0)))
        pair = jnp.where(code == 3, 6, jnp.where(code == 4, 10, jnp.where(code == 5, 12, pair)))
        wide = jnp.dot(pair.astype(F32).astype(BF), spread, preferred_element_type=F32).astype(jnp.int32)
        kept = ((wide >> place) & 1).astype(F32) * UPDATE_SCALE
        mask_ref[:, block * 512 : (block + 1) * 512] = kept.astype(BF)


def first_kernel(block_ref, grad_ref, down_ref, up_ref):
    for matrix in range(MATS_HERE):
        down_ref[matrix] = grad_ref[block_ref[0] * MATS_HERE + matrix]
        up_ref[matrix] = grad_ref[block_ref[1] * MATS_HERE + matrix]


def add_kernel(block_ref, grad_ref, received_ref, total_ref):
    for matrix in range(MATS_HERE):
        total_ref[matrix] = received_ref[matrix] + grad_ref[block_ref[0] * MATS_HERE + matrix]


def momentum_kernel(block_ref, grad_ref, down_ref, up_ref, momentum_ref, next_ref, out_ref):
    for matrix in range(MATS_HERE):
        own = grad_ref[block_ref[0] * MATS_HERE + matrix].astype(F32)
        summed = down_ref[matrix].astype(F32) + up_ref[matrix].astype(F32) + own
        value = DECAY_RATE * momentum_ref[matrix] + summed
        next_ref[matrix] = value
        out_ref[matrix] = value.astype(BF)


def split(value):
    high = value.astype(BF)
    return high, (value - high.astype(F32)).astype(BF)


def product(left, right, dims=(((1,), (0,)), ((), ()))):
    def one(a, b):
        return lax.dot_general(a, b, dims, preferred_element_type=F32)

    return one(left[0], right[0]) + (one(left[0], right[1]) + one(left[1], right[0]))


def orthogonal_kernel(place_ref, mine_ref, other_ref, out_ref, coef_ref):
    mine = mine_ref[...]
    other = other_ref[...]

    def block(a, b):
        return lax.dot_general(a, b, NT, preferred_element_type=F32)

    cross = block(mine, other)
    gram = jnp.concatenate(
        [
            jnp.concatenate([block(mine, mine), cross], axis=1),
            jnp.concatenate([cross.T, block(other, other)], axis=1),
        ],
        axis=0,
    )
    diagonal = lax.broadcasted_iota(jnp.int32, (ROWS, ROWS), 0) == lax.broadcasted_iota(jnp.int32, (ROWS, ROWS), 1)
    trace_sum = jnp.sum(jnp.where(diagonal, gram, 0.0))
    inverse = lax.rsqrt(jnp.full((1, 1), trace_sum + EPSILON, F32))
    scaled = gram * (inverse * inverse)
    first = jnp.where(diagonal, QUINTIC_FIRST, 0.0)
    square_form = scaled
    factor = None
    factor_scaled = split(scaled)
    for iteration in range(ITERS):
        parts = split(square_form)
        polynomial = split(first + QUINTIC_SECOND * square_form + QUINTIC_THIRD * product(parts, parts))
        factor = polynomial if factor is None else split(product(polynomial, factor))
        if iteration + 1 < ITERS:
            factor_scaled = split(product(polynomial, factor_scaled))
            square_form = product(factor_scaled, factor, NT)
    coef_ref[...] = (factor[0].astype(F32) + factor[1].astype(F32)) * inverse
    rows = pl.ds(pl.multiple_of(place_ref[0] * OWN_ROWS, OWN_ROWS), OWN_ROWS)
    coef = coef_ref[rows, :].astype(BF)
    out_ref[...] = (
        jnp.dot(coef[:, :HALF], mine, preferred_element_type=F32)
        + jnp.dot(coef[:, HALF:], other, preferred_element_type=F32)
    ).astype(BF)


def update_kernel(returned_ref, mask_ref, update_ref):
    for matrix in range(MATS_HERE):
        update_ref[matrix] = returned_ref[matrix] * mask_ref[matrix]


def call(kernel, outs, *args, scalars=0, scratch=()):
    return pl.pallas_call(
        kernel,
        out_shape=outs,
        in_specs=[smem() if i < scalars else vmem() for i in range(len(args))],
        out_specs=jax.tree.map(lambda _: vmem(), outs),
        scratch_shapes=list(scratch),
        compiler_params=PARAMS,
    )(*args)


def shaped(shape, dtype):
    return jax.ShapeDtypeStruct(shape, dtype)


def local(grad_parts, momentum, mask_codes):
    reps = lax.axis_size("rep")
    place = lax.axis_index("rep")
    grads = grad_parts[0]
    chunk = shaped(CHUNK, BF)

    def block(offset):
        return lax.rem(place + (offset + reps), reps).astype(jnp.int32).reshape(1)

    def send(value, step):
        return lax.ppermute(value, "rep", [(i, (i + step) % reps) for i in range(reps)])

    below = reps // 2
    above = reps - 1 - below
    down, up = call(first_kernel, (chunk, chunk), jnp.concatenate([block(-below), block(above)]), grads, scalars=1)
    down, up = send(down, -1), send(up, 1)
    codes = mask_codes.reshape(MATS_HERE * PIECE_ROWS, COLS // 4)
    for step in range(1, below):
        down = send(call(add_kernel, chunk, block(step - below), grads, down, scalars=1), -1)
        if step < above:
            up = send(call(add_kernel, chunk, block(above - step), grads, up, scalars=1), 1)
        if step == 2:
            up, codes = lax.optimization_barrier((up, codes))
    mask = call(mask_kernel, shaped((MATS_HERE * PIECE_ROWS, COLS), BF), codes).reshape(CHUNK)
    down, up, mask = lax.optimization_barrier((down, up, mask))
    momentum_next, outgoing = call(
        momentum_kernel, (shaped(CHUNK, F32), chunk), block(0), grads, down, up, momentum, scalars=1
    )
    pieces = lax.all_to_all(
        outgoing, "shard", split_axis=0, concat_axis=0, tiled=True, axis_index_groups=GROUPS_Y
    ).reshape(OWN_ROWS, COLS)
    mine = lax.all_gather(pieces, "shard", axis=0, tiled=True, axis_index_groups=GROUPS_X)
    other = lax.ppermute(mine, "shard", OTHER_CORE)
    own_place = (lax.axis_index("shard") // (PLANE_Y * CORES)).astype(jnp.int32).reshape(1)
    orthogonal = call(
        orthogonal_kernel,
        shaped((OWN_ROWS, COLS), BF),
        own_place,
        mine,
        other,
        scalars=1,
        scratch=[pltpu.VMEM((ROWS, ROWS), F32)],
    )
    returned = lax.all_to_all(
        orthogonal.reshape(CHUNK), "shard", split_axis=0, concat_axis=0, tiled=True, axis_index_groups=GROUPS_Y
    )
    update = call(update_kernel, chunk, returned, mask)
    return (momentum_next, update)


def solution(mesh):
    in_specs = (P("rep", None, "shard", None), P("rep", "shard", None), P("rep", "shard", None))
    out_specs = (P("rep", "shard", None), P("rep", "shard", None))
    return jax.shard_map(local, mesh=mesh, in_specs=in_specs, out_specs=out_specs, check_vma=False)
```

```python
import functools

import jax
import jax.numpy as jnp
from jax import lax
from jax.experimental import pallas as pl
from jax.experimental.pallas import tpu as pltpu
from jax.sharding import PartitionSpec as P

ITERS = 5
DECAY_RATE = 0.95
EPSILON = 1e-07
QUINTIC_FIRST = 3.4445
QUINTIC_SECOND = -4.775
QUINTIC_THIRD = 2.0315
UPDATE_SCALE = 64.0

REPS = 12
MATS_HERE = 8
PIECE_ROWS = 4
COLS = 3584
ROWS = 256
HALF = ROWS // 2
PLANE_X = 4
PLANE_Y = 8
CORES = 2
SHARDS = PLANE_X * PLANE_Y * CORES
OWN_ROWS = PLANE_Y * PIECE_ROWS
BF = jnp.bfloat16
F32 = jnp.float32
CHUNK = (MATS_HERE, PIECE_ROWS, COLS)
PARAMS = pltpu.CompilerParams(vmem_limit_bytes=8 * 1024 * 1024)
NT = (((1,), (1,)), ((), ()))


def shard_index(x, y, core):
    return (x * PLANE_Y + y) * CORES + core


GROUPS_Y = [[shard_index(x, y, c) for y in range(PLANE_Y)] for x in range(PLANE_X) for c in range(CORES)]
GROUPS_X = [[shard_index(x, y, c) for x in range(PLANE_X)] for y in range(PLANE_Y) for c in range(CORES)]
OTHER_CORE = [(i, i ^ 1) for i in range(SHARDS)]


def vmem():
    return pl.BlockSpec(memory_space=pltpu.VMEM)


def smem():
    return pl.BlockSpec(memory_space=pltpu.SMEM)


def mask_kernel(codes_ref, mask_ref):
    group = lax.broadcasted_iota(jnp.int32, (128, 512), 0)
    column = lax.broadcasted_iota(jnp.int32, (128, 512), 1)
    spread = jnp.where((column >> 2) == group, 1.0, 0.0).astype(BF)
    place = lax.broadcasted_iota(jnp.int32, (32, 512), 1) & 3
    for block in range(7):
        code = codes_ref[:, block * 128 : (block + 1) * 128]
        pair = jnp.where(code == 0, 3, jnp.where(code == 1, 5, jnp.where(code == 2, 9, 0)))
        pair = jnp.where(code == 3, 6, jnp.where(code == 4, 10, jnp.where(code == 5, 12, pair)))
        wide = jnp.dot(pair.astype(F32).astype(BF), spread, preferred_element_type=F32).astype(jnp.int32)
        kept = ((wide >> place) & 1).astype(F32) * UPDATE_SCALE
        mask_ref[:, block * 512 : (block + 1) * 512] = kept.astype(BF)


def grad_chunk(blocks_ref, grad_ref, offset, matrix):
    return grad_ref[blocks_ref[offset % REPS] * MATS_HERE + matrix]


def first_kernel(below, above, blocks_ref, grad_ref, down_ref, up_ref):
    for matrix in range(MATS_HERE):
        down_ref[matrix] = grad_chunk(blocks_ref, grad_ref, below, matrix)
        up_ref[matrix] = grad_chunk(blocks_ref, grad_ref, above, matrix)


def add_kernel(offset, blocks_ref, grad_ref, received_ref, total_ref):
    for matrix in range(MATS_HERE):
        total_ref[matrix] = received_ref[matrix] + grad_chunk(blocks_ref, grad_ref, offset, matrix)


def momentum_kernel(blocks_ref, grad_ref, down_ref, up_ref, momentum_ref, next_ref, out_ref):
    for matrix in range(MATS_HERE):
        own = grad_chunk(blocks_ref, grad_ref, 0, matrix).astype(F32)
        summed = down_ref[matrix].astype(F32) + up_ref[matrix].astype(F32) + own
        value = DECAY_RATE * momentum_ref[matrix] + summed
        next_ref[matrix] = value
        out_ref[matrix] = value.astype(BF)


def split(value):
    high = value.astype(BF)
    return high, (value - high.astype(F32)).astype(BF)


def product(left, right, dims=(((1,), (0,)), ((), ()))):
    def one(a, b):
        return lax.dot_general(a, b, dims, preferred_element_type=F32)

    return one(left[0], right[0]) + (one(left[0], right[1]) + one(left[1], right[0]))


def orthogonal_kernel(place_ref, mine_ref, other_ref, out_ref, coef_ref):
    mine = mine_ref[...]
    other = other_ref[...]

    def block(a, b):
        return lax.dot_general(a, b, NT, preferred_element_type=F32)

    cross = block(mine, other)
    gram = jnp.concatenate(
        [
            jnp.concatenate([block(mine, mine), cross], axis=1),
            jnp.concatenate([cross.T, block(other, other)], axis=1),
        ],
        axis=0,
    )
    diagonal = lax.broadcasted_iota(jnp.int32, (ROWS, ROWS), 0) == lax.broadcasted_iota(jnp.int32, (ROWS, ROWS), 1)
    trace_sum = jnp.sum(jnp.where(diagonal, gram, 0.0))
    inverse = lax.rsqrt(jnp.full((1, 1), trace_sum + EPSILON, F32))
    scaled = gram * (inverse * inverse)
    first = jnp.where(diagonal, QUINTIC_FIRST, 0.0)
    square_form = scaled
    factor = None
    factor_scaled = split(scaled)
    for iteration in range(ITERS):
        parts = split(square_form)
        polynomial = split(first + QUINTIC_SECOND * square_form + QUINTIC_THIRD * product(parts, parts))
        factor = polynomial if factor is None else split(product(polynomial, factor))
        if iteration + 1 < ITERS:
            factor_scaled = split(product(polynomial, factor_scaled))
            square_form = product(factor_scaled, factor, NT)
    coef_ref[...] = (factor[0].astype(F32) + factor[1].astype(F32)) * inverse
    rows = pl.ds(pl.multiple_of(place_ref[0] * OWN_ROWS, OWN_ROWS), OWN_ROWS)
    coef = coef_ref[rows, :].astype(BF)
    out_ref[...] = (
        jnp.dot(coef[:, :HALF], mine, preferred_element_type=F32)
        + jnp.dot(coef[:, HALF:], other, preferred_element_type=F32)
    ).astype(BF)


def update_kernel(returned_ref, mask_ref, update_ref):
    for matrix in range(MATS_HERE):
        update_ref[matrix] = returned_ref[matrix] * mask_ref[matrix]


def call(kernel, outs, *args, scalars=0, scratch=()):
    return pl.pallas_call(
        kernel,
        out_shape=outs,
        in_specs=[smem() if i < scalars else vmem() for i in range(len(args))],
        out_specs=jax.tree.map(lambda _: vmem(), outs),
        scratch_shapes=list(scratch),
        compiler_params=PARAMS,
    )(*args)


def shaped(shape, dtype):
    return jax.ShapeDtypeStruct(shape, dtype)


def local(grad_parts, momentum, mask_codes):
    grads = grad_parts[0]
    chunk = shaped(CHUNK, BF)
    blocks = lax.rem(lax.axis_index("rep") + lax.iota(jnp.int32, REPS), REPS)

    def send(value, step):
        return lax.ppermute(value, "rep", [(i, (i + step) % REPS) for i in range(REPS)])

    def add(offset, received):
        return call(functools.partial(add_kernel, offset), chunk, blocks, grads, received, scalars=1)

    below = REPS // 2
    above = REPS - 1 - below
    down, up = call(functools.partial(first_kernel, -below, above), (chunk, chunk), blocks, grads, scalars=1)
    down, up = send(down, -1), send(up, 1)
    for step in range(1, below):
        down = send(add(step - below, down), -1)
        if step < above:
            up = send(add(above - step, up), 1)
    momentum_next, outgoing = call(
        momentum_kernel, (shaped(CHUNK, F32), chunk), blocks, grads, down, up, momentum, scalars=1
    )
    pieces = lax.all_to_all(
        outgoing, "shard", split_axis=0, concat_axis=0, tiled=True, axis_index_groups=GROUPS_Y
    ).reshape(OWN_ROWS, COLS)
    mine = lax.all_gather(pieces, "shard", axis=0, tiled=True, axis_index_groups=GROUPS_X)
    mine, codes = lax.optimization_barrier((mine, mask_codes))
    other = lax.ppermute(mine, "shard", OTHER_CORE)
    mask = call(
        mask_kernel,
        shaped((MATS_HERE * PIECE_ROWS, COLS), BF),
        codes.reshape(MATS_HERE * PIECE_ROWS, COLS // 4),
    ).reshape(CHUNK)
    other, mask = lax.optimization_barrier((other, mask))
    own_place = (lax.axis_index("shard") // (PLANE_Y * CORES)).astype(jnp.int32).reshape(1)
    orthogonal = call(
        orthogonal_kernel,
        shaped((OWN_ROWS, COLS), BF),
        own_place,
        mine,
        other,
        scalars=1,
        scratch=[pltpu.VMEM((ROWS, ROWS), F32)],
    )
    returned = lax.all_to_all(
        orthogonal.reshape(CHUNK), "shard", split_axis=0, concat_axis=0, tiled=True, axis_index_groups=GROUPS_Y
    )
    update = call(update_kernel, chunk, returned, mask)
    return (momentum_next, update)


def solution(mesh):
    in_specs = (P("rep", None, "shard", None), P("rep", "shard", None), P("rep", "shard", None))
    out_specs = (P("rep", "shard", None), P("rep", "shard", None))
    return jax.shard_map(local, mesh=mesh, in_specs=in_specs, out_specs=out_specs, check_vma=False)
```

```python
import functools

import jax
import jax.numpy as jnp
from jax import lax
from jax.experimental import pallas as pl
from jax.experimental.pallas import tpu as pltpu
from jax.sharding import PartitionSpec as P

ITERS = 5
DECAY_RATE = 0.95
EPSILON = 1e-07
QUINTIC_FIRST = 3.4445
QUINTIC_SECOND = -4.775
QUINTIC_THIRD = 2.0315
UPDATE_SCALE = 64.0

REPS = 12
MATS_HERE = 8
PIECE_ROWS = 4
COLS = 3584
ROWS = 256
HALF = ROWS // 2
PLANE_X = 4
PLANE_Y = 8
CORES = 2
SHARDS = PLANE_X * PLANE_Y * CORES
OWN_ROWS = PLANE_Y * PIECE_ROWS
BF = jnp.bfloat16
F32 = jnp.float32
CHUNK = (MATS_HERE, PIECE_ROWS, COLS)
TILES = COLS // 512
VIEW = (MATS_HERE * TILES, 4 * PIECE_ROWS, 128)
PARAMS = pltpu.CompilerParams(vmem_limit_bytes=8 * 1024 * 1024)
NT = (((1,), (1,)), ((), ()))


def shard_index(x, y, core):
    return (x * PLANE_Y + y) * CORES + core


GROUPS_Y = [[shard_index(x, y, c) for y in range(PLANE_Y)] for x in range(PLANE_X) for c in range(CORES)]
GROUPS_X = [[shard_index(x, y, c) for x in range(PLANE_X)] for y in range(PLANE_Y) for c in range(CORES)]
OTHER_CORE = [(i, i ^ 1) for i in range(SHARDS)]


def vmem():
    return pl.BlockSpec(memory_space=pltpu.VMEM)


def smem():
    return pl.BlockSpec(memory_space=pltpu.SMEM)


def mask_kernel(codes_ref, mask_ref):
    group = lax.broadcasted_iota(jnp.int32, (128, 512), 0)
    column = lax.broadcasted_iota(jnp.int32, (128, 512), 1)
    spread = jnp.where((column >> 2) == group, 1.0, 0.0).astype(BF)
    place = lax.broadcasted_iota(jnp.int32, (32, 512), 1) & 3
    for block in range(7):
        code = codes_ref[:, block * 128 : (block + 1) * 128]
        pair = jnp.where(code == 0, 3, jnp.where(code == 1, 5, jnp.where(code == 2, 9, 0)))
        pair = jnp.where(code == 3, 6, jnp.where(code == 4, 10, jnp.where(code == 5, 12, pair)))
        wide = jnp.dot(pair.astype(F32).astype(BF), spread, preferred_element_type=F32).astype(jnp.int32)
        kept = ((wide >> place) & 1).astype(F32) * UPDATE_SCALE
        mask_ref[:, block * 512 : (block + 1) * 512] = kept.astype(BF)


def as_tiles(array):
    split_up = array.reshape(-1, PIECE_ROWS, TILES, 4, 128)
    return split_up.transpose(0, 2, 3, 1, 4).reshape(-1, 4 * PIECE_ROWS, 128)


def as_rows(tiles):
    split_up = tiles.reshape(-1, TILES, 4, PIECE_ROWS, 128)
    return split_up.transpose(0, 3, 1, 2, 4).reshape(-1, PIECE_ROWS, COLS)


def grad_chunk(blocks_ref, grad_ref, offset):
    return grad_ref.at[pl.ds(blocks_ref[offset % REPS] * VIEW[0], VIEW[0])]


def first_kernel(below, above, blocks_ref, grad_ref, down_ref, up_ref, sems):
    copies = [
        pltpu.make_async_copy(grad_chunk(blocks_ref, grad_ref, below), down_ref, sems.at[0]),
        pltpu.make_async_copy(grad_chunk(blocks_ref, grad_ref, above), up_ref, sems.at[1]),
    ]
    for copy in copies:
        copy.start()
    for copy in copies:
        copy.wait()


def add_kernel(offset, blocks_ref, grad_ref, received_ref, total_ref):
    total_ref[...] = received_ref[...] + grad_chunk(blocks_ref, grad_ref, offset)[...]


def summed_momentum(blocks_ref, grad_ref, down_ref, up_ref, momentum_ref):
    own = grad_chunk(blocks_ref, grad_ref, 0)[...].astype(F32)
    summed = down_ref[...].astype(F32) + up_ref[...].astype(F32) + own
    return DECAY_RATE * momentum_ref[...] + summed


def outgoing_kernel(blocks_ref, grad_ref, down_ref, up_ref, momentum_ref, out_ref):
    out_ref[...] = summed_momentum(blocks_ref, grad_ref, down_ref, up_ref, momentum_ref).astype(BF)


def momentum_kernel(blocks_ref, grad_ref, down_ref, up_ref, momentum_ref, next_ref):
    next_ref[...] = summed_momentum(blocks_ref, grad_ref, down_ref, up_ref, momentum_ref)


def split(value):
    high = value.astype(BF)
    return high, (value - high.astype(F32)).astype(BF)


def product(left, right, dims=(((1,), (0,)), ((), ()))):
    def one(a, b):
        return lax.dot_general(a, b, dims, preferred_element_type=F32)

    return one(left[0], right[0]) + (one(left[0], right[1]) + one(left[1], right[0]))


def orthogonal_kernel(place_ref, mine_ref, other_ref, out_ref, coef_ref):
    mine = mine_ref[...]
    other = other_ref[...]

    def block(a, b):
        return lax.dot_general(a, b, NT, preferred_element_type=F32)

    cross = block(mine, other)
    gram = jnp.concatenate(
        [
            jnp.concatenate([block(mine, mine), cross], axis=1),
            jnp.concatenate([cross.T, block(other, other)], axis=1),
        ],
        axis=0,
    )
    diagonal = lax.broadcasted_iota(jnp.int32, (ROWS, ROWS), 0) == lax.broadcasted_iota(jnp.int32, (ROWS, ROWS), 1)
    trace_sum = jnp.sum(jnp.where(diagonal, gram, 0.0))
    inverse = lax.rsqrt(jnp.full((1, 1), trace_sum + EPSILON, F32))
    scaled = gram * (inverse * inverse)
    first = jnp.where(diagonal, QUINTIC_FIRST, 0.0)
    square_form = scaled
    factor = None
    factor_scaled = split(scaled)
    for iteration in range(ITERS):
        parts = split(square_form)
        polynomial = split(first + QUINTIC_SECOND * square_form + QUINTIC_THIRD * product(parts, parts))
        factor = polynomial if factor is None else split(product(polynomial, factor))
        if iteration + 1 < ITERS:
            factor_scaled = split(product(polynomial, factor_scaled))
            square_form = product(factor_scaled, factor, NT)
    coef_ref[...] = (factor[0].astype(F32) + factor[1].astype(F32)) * inverse
    rows = pl.ds(pl.multiple_of(place_ref[0] * OWN_ROWS, OWN_ROWS), OWN_ROWS)
    coef = coef_ref[rows, :].astype(BF)
    out_ref[...] = (
        jnp.dot(coef[:, :HALF], mine, preferred_element_type=F32)
        + jnp.dot(coef[:, HALF:], other, preferred_element_type=F32)
    ).astype(BF)


def update_kernel(returned_ref, mask_ref, update_ref):
    update_ref[...] = returned_ref[...] * mask_ref[...]


def call(kernel, outs, *args, scalars=0, scratch=(), in_hbm=()):
    def place(index):
        if index < scalars:
            return smem()
        return pl.BlockSpec(memory_space=pltpu.HBM) if index in in_hbm else vmem()

    return pl.pallas_call(
        kernel,
        out_shape=outs,
        in_specs=[place(i) for i in range(len(args))],
        out_specs=jax.tree.map(lambda _: vmem(), outs),
        scratch_shapes=list(scratch),
        compiler_params=PARAMS,
    )(*args)


def shaped(shape, dtype):
    return jax.ShapeDtypeStruct(shape, dtype)


def local(grad_parts, momentum, mask_codes):
    grads = as_tiles(grad_parts[0])
    momentum = as_tiles(momentum)
    chunk = shaped(VIEW, BF)
    blocks = lax.rem(lax.axis_index("rep") + lax.iota(jnp.int32, REPS), REPS)

    def send(value, step):
        return lax.ppermute(value, "rep", [(i, (i + step) % REPS) for i in range(REPS)])

    def add(offset, received):
        return call(functools.partial(add_kernel, offset), chunk, blocks, grads, received, scalars=1)

    below = REPS // 2
    above = REPS - 1 - below
    down, up = call(
        functools.partial(first_kernel, -below, above),
        (chunk, chunk),
        blocks,
        grads,
        scalars=1,
        in_hbm=(1,),
        scratch=[pltpu.SemaphoreType.DMA((2,))],
    )
    down, up = send(down, -1), send(up, 1)
    for step in range(1, below):
        down = send(add(step - below, down), -1)
        if step < above:
            up = send(add(above - step, up), 1)
    parts = (blocks, grads, down, up, momentum)
    outgoing = as_rows(call(outgoing_kernel, chunk, *parts, scalars=1))
    pieces = lax.all_to_all(
        outgoing, "shard", split_axis=0, concat_axis=0, tiled=True, axis_index_groups=GROUPS_Y
    ).reshape(OWN_ROWS, COLS)
    mine = lax.all_gather(pieces, "shard", axis=0, tiled=True, axis_index_groups=GROUPS_X)
    mine, codes, parts = lax.optimization_barrier((mine, mask_codes, parts))
    other = lax.ppermute(mine, "shard", OTHER_CORE)
    mask = call(
        mask_kernel,
        shaped((MATS_HERE * PIECE_ROWS, COLS), BF),
        codes.reshape(MATS_HERE * PIECE_ROWS, COLS // 4),
    ).reshape(CHUNK)
    momentum_next = call(momentum_kernel, shaped(VIEW, F32), *parts, scalars=1)
    other, mask, momentum_next = lax.optimization_barrier((other, mask, momentum_next))
    own_place = (lax.axis_index("shard") // (PLANE_Y * CORES)).astype(jnp.int32).reshape(1)
    orthogonal = call(
        orthogonal_kernel,
        shaped((OWN_ROWS, COLS), BF),
        own_place,
        mine,
        other,
        scalars=1,
        scratch=[pltpu.VMEM((ROWS, ROWS), F32)],
    )
    returned = lax.all_to_all(
        orthogonal.reshape(CHUNK), "shard", split_axis=0, concat_axis=0, tiled=True, axis_index_groups=GROUPS_Y
    )
    update = call(update_kernel, chunk, as_tiles(returned), as_tiles(mask))
    return (as_rows(momentum_next), as_rows(update))


def solution(mesh):
    in_specs = (P("rep", None, "shard", None), P("rep", "shard", None), P("rep", "shard", None))
    out_specs = (P("rep", "shard", None), P("rep", "shard", None))
    return jax.shard_map(local, mesh=mesh, in_specs=in_specs, out_specs=out_specs, check_vma=False)
```

```python
import functools

import jax
import jax.numpy as jnp
from jax import lax
from jax.experimental import pallas as pl
from jax.experimental.pallas import tpu as pltpu
from jax.sharding import PartitionSpec as P

ITERS = 5
DECAY_RATE = 0.95
EPSILON = 1e-07
QUINTIC_FIRST = 3.4445
QUINTIC_SECOND = -4.775
QUINTIC_THIRD = 2.0315
UPDATE_SCALE = 64.0

REPS = 12
MATS_HERE = 8
PIECE_ROWS = 4
COLS = 3584
ROWS = 256
HALF = ROWS // 2
PLANE_X = 4
PLANE_Y = 8
CORES = 2
SHARDS = PLANE_X * PLANE_Y * CORES
OWN_ROWS = PLANE_Y * PIECE_ROWS
BF = jnp.bfloat16
F32 = jnp.float32
CHUNK = (MATS_HERE, PIECE_ROWS, COLS)
PARAMS = pltpu.CompilerParams(vmem_limit_bytes=8 * 1024 * 1024)
NT = (((1,), (1,)), ((), ()))


def shard_index(x, y, core):
    return (x * PLANE_Y + y) * CORES + core


GROUPS_Y = [[shard_index(x, y, c) for y in range(PLANE_Y)] for x in range(PLANE_X) for c in range(CORES)]
GROUPS_X = [[shard_index(x, y, c) for x in range(PLANE_X)] for y in range(PLANE_Y) for c in range(CORES)]
OTHER_CORE = [(i, i ^ 1) for i in range(SHARDS)]


def vmem():
    return pl.BlockSpec(memory_space=pltpu.VMEM)


def mask_kernel(codes_ref, mask_ref):
    group = lax.broadcasted_iota(jnp.int32, (128, 512), 0)
    column = lax.broadcasted_iota(jnp.int32, (128, 512), 1)
    spread = jnp.where((column >> 2) == group, 1.0, 0.0).astype(BF)
    place = lax.broadcasted_iota(jnp.int32, (32, 512), 1) & 3
    for block in range(7):
        code = codes_ref[:, block * 128 : (block + 1) * 128]
        pair = jnp.where(code == 0, 3, jnp.where(code == 1, 5, jnp.where(code == 2, 9, 0)))
        pair = jnp.where(code == 3, 6, jnp.where(code == 4, 10, jnp.where(code == 5, 12, pair)))
        wide = jnp.dot(pair.astype(F32).astype(BF), spread, preferred_element_type=F32).astype(jnp.int32)
        kept = ((wide >> place) & 1).astype(F32) * UPDATE_SCALE
        mask_ref[:, block * 512 : (block + 1) * 512] = kept.astype(BF)


def chunk_start(offset):
    place = lax.rem(lax.axis_index("rep") + offset % REPS, REPS)
    return place * MATS_HERE


def first_kernel(below, above, grad_ref, down_ref, up_ref):
    start_down, start_up = chunk_start(below), chunk_start(above)
    for matrix in range(MATS_HERE):
        down_ref[matrix] = grad_ref[start_down + matrix]
        up_ref[matrix] = grad_ref[start_up + matrix]


def add_kernel(offset, grad_ref, received_ref, total_ref):
    start = chunk_start(offset)
    for matrix in range(MATS_HERE):
        total_ref[matrix] = received_ref[matrix] + grad_ref[start + matrix]


def momentum_kernel(grad_ref, down_ref, up_ref, momentum_ref, next_ref, out_ref):
    start = chunk_start(0)
    for matrix in range(MATS_HERE):
        own = grad_ref[start + matrix].astype(F32)
        summed = down_ref[matrix].astype(F32) + up_ref[matrix].astype(F32) + own
        value = DECAY_RATE * momentum_ref[matrix] + summed
        next_ref[matrix] = value
        out_ref[matrix] = value.astype(BF)


def split(value):
    high = value.astype(BF)
    return high, (value - high.astype(F32)).astype(BF)


def product(left, right, dims=(((1,), (0,)), ((), ()))):
    def one(a, b):
        return lax.dot_general(a, b, dims, preferred_element_type=F32)

    return one(left[0], right[0]) + (one(left[0], right[1]) + one(left[1], right[0]))


def orthogonal_kernel(mine_ref, other_ref, out_ref, coef_ref):
    mine = mine_ref[...]
    other = other_ref[...]

    def block(a, b):
        return lax.dot_general(a, b, NT, preferred_element_type=F32)

    cross = block(mine, other)
    gram = jnp.concatenate(
        [
            jnp.concatenate([block(mine, mine), cross], axis=1),
            jnp.concatenate([cross.T, block(other, other)], axis=1),
        ],
        axis=0,
    )
    diagonal = lax.broadcasted_iota(jnp.int32, (ROWS, ROWS), 0) == lax.broadcasted_iota(jnp.int32, (ROWS, ROWS), 1)
    trace_sum = jnp.sum(jnp.where(diagonal, gram, 0.0))
    inverse = lax.rsqrt(jnp.full((1, 1), trace_sum + EPSILON, F32))
    scaled = gram * (inverse * inverse)
    first = jnp.where(diagonal, QUINTIC_FIRST, 0.0)
    square_form = scaled
    factor = None
    factor_scaled = split(scaled)
    for iteration in range(ITERS):
        parts = split(square_form)
        polynomial = split(first + QUINTIC_SECOND * square_form + QUINTIC_THIRD * product(parts, parts))
        factor = polynomial if factor is None else split(product(polynomial, factor))
        if iteration + 1 < ITERS:
            factor_scaled = split(product(polynomial, factor_scaled))
            square_form = product(factor_scaled, factor, NT)
    coef_ref[...] = (factor[0].astype(F32) + factor[1].astype(F32)) * inverse
    place_x = lax.div(lax.axis_index("shard"), PLANE_Y * CORES)
    rows = pl.ds(pl.multiple_of(place_x * OWN_ROWS, OWN_ROWS), OWN_ROWS)
    coef = coef_ref[rows, :].astype(BF)
    out_ref[...] = (
        jnp.dot(coef[:, :HALF], mine, preferred_element_type=F32)
        + jnp.dot(coef[:, HALF:], other, preferred_element_type=F32)
    ).astype(BF)


def update_kernel(returned_ref, mask_ref, update_ref):
    for matrix in range(MATS_HERE):
        update_ref[matrix] = returned_ref[matrix] * mask_ref[matrix]


def call(kernel, outs, *args, scratch=()):
    return pl.pallas_call(
        kernel,
        out_shape=outs,
        in_specs=[vmem() for _ in args],
        out_specs=jax.tree.map(lambda _: vmem(), outs),
        scratch_shapes=list(scratch),
        compiler_params=PARAMS,
    )(*args)


def shaped(shape, dtype):
    return jax.ShapeDtypeStruct(shape, dtype)


def local(grad_parts, momentum, mask_codes):
    grads = grad_parts[0]
    chunk = shaped(CHUNK, BF)

    def send(value, step):
        return lax.ppermute(value, "rep", [(i, (i + step) % REPS) for i in range(REPS)])

    def add(offset, received):
        return call(functools.partial(add_kernel, offset), chunk, grads, received)

    below = REPS // 2
    above = REPS - 1 - below
    down, up = call(functools.partial(first_kernel, -below, above), (chunk, chunk), grads)
    down, up = send(down, -1), send(up, 1)
    for step in range(1, below):
        down = send(add(step - below, down), -1)
        if step < above:
            up = send(add(above - step, up), 1)
    momentum_next, outgoing = call(momentum_kernel, (shaped(CHUNK, F32), chunk), grads, down, up, momentum)
    pieces = lax.all_to_all(
        outgoing, "shard", split_axis=0, concat_axis=0, tiled=True, axis_index_groups=GROUPS_Y
    ).reshape(OWN_ROWS, COLS)
    mine = lax.all_gather(pieces, "shard", axis=0, tiled=True, axis_index_groups=GROUPS_X)
    mine, codes = lax.optimization_barrier((mine, mask_codes))
    other = lax.ppermute(mine, "shard", OTHER_CORE)
    mask = call(
        mask_kernel,
        shaped((MATS_HERE * PIECE_ROWS, COLS), BF),
        codes.reshape(MATS_HERE * PIECE_ROWS, COLS // 4),
    ).reshape(CHUNK)
    other, mask = lax.optimization_barrier((other, mask))
    orthogonal = call(
        orthogonal_kernel,
        shaped((OWN_ROWS, COLS), BF),
        mine,
        other,
        scratch=[pltpu.VMEM((ROWS, ROWS), F32)],
    )
    returned = lax.all_to_all(
        orthogonal.reshape(CHUNK), "shard", split_axis=0, concat_axis=0, tiled=True, axis_index_groups=GROUPS_Y
    )
    update = call(update_kernel, chunk, returned, mask)
    return (momentum_next, update)


def solution(mesh):
    in_specs = (P("rep", None, "shard", None), P("rep", "shard", None), P("rep", "shard", None))
    out_specs = (P("rep", "shard", None), P("rep", "shard", None))
    return jax.shard_map(local, mesh=mesh, in_specs=in_specs, out_specs=out_specs, check_vma=False)
```

```python
import functools

import jax
import jax.numpy as jnp
from jax import lax
from jax.experimental import pallas as pl
from jax.experimental.pallas import tpu as pltpu
from jax.sharding import PartitionSpec as P

ITERS = 5
DECAY_RATE = 0.95
EPSILON = 1e-07
QUINTIC_FIRST = 3.4445
QUINTIC_SECOND = -4.775
QUINTIC_THIRD = 2.0315
UPDATE_SCALE = 64.0

REPS = 12
MATS_HERE = 8
PIECE_ROWS = 4
COLS = 3584
ROWS = 256
HALF = ROWS // 2
PLANE_X = 4
PLANE_Y = 8
CORES = 2
SHARDS = PLANE_X * PLANE_Y * CORES
OWN_ROWS = PLANE_Y * PIECE_ROWS
BF = jnp.bfloat16
F32 = jnp.float32
CHUNK = (MATS_HERE, PIECE_ROWS, COLS)
PARAMS = pltpu.CompilerParams(vmem_limit_bytes=8 * 1024 * 1024)
NT = (((1,), (1,)), ((), ()))


def shard_index(x, y, core):
    return (x * PLANE_Y + y) * CORES + core


GROUPS_Y = [[shard_index(x, y, c) for y in range(PLANE_Y)] for x in range(PLANE_X) for c in range(CORES)]
GROUPS_X = [[shard_index(x, y, c) for x in range(PLANE_X)] for y in range(PLANE_Y) for c in range(CORES)]
OTHER_CORE = [(i, i ^ 1) for i in range(SHARDS)]


def vmem():
    return pl.BlockSpec(memory_space=pltpu.VMEM)


def mask_kernel(codes_ref, mask_ref):
    group = lax.broadcasted_iota(jnp.int32, (128, 512), 0)
    column = lax.broadcasted_iota(jnp.int32, (128, 512), 1)
    spread = jnp.where((column >> 2) == group, 1.0, 0.0).astype(BF)
    place = lax.broadcasted_iota(jnp.int32, (MATS_HERE * PIECE_ROWS, 512), 1) & 3
    for block in range(7):
        here = slice(block * 128, (block + 1) * 128)
        code = jnp.concatenate([codes_ref[matrix, :, here] for matrix in range(MATS_HERE)], axis=0)
        pair = jnp.where(code == 0, 3, jnp.where(code == 1, 5, jnp.where(code == 2, 9, 0)))
        pair = jnp.where(code == 3, 6, jnp.where(code == 4, 10, jnp.where(code == 5, 12, pair)))
        wide = jnp.dot(pair.astype(F32).astype(BF), spread, preferred_element_type=F32).astype(jnp.int32)
        kept = ((wide >> place) & 1).astype(F32) * UPDATE_SCALE
        for matrix in range(MATS_HERE):
            rows = kept[matrix * PIECE_ROWS : (matrix + 1) * PIECE_ROWS]
            mask_ref[matrix, :, block * 512 : (block + 1) * 512] = rows.astype(BF)


def chunk_start(offset):
    place = lax.rem(lax.axis_index("rep") + offset % REPS, REPS)
    return place * MATS_HERE


def first_kernel(below, above, grad_ref, down_ref, up_ref):
    start_down, start_up = chunk_start(below), chunk_start(above)
    for matrix in range(MATS_HERE):
        down_ref[matrix] = grad_ref[start_down + matrix]
        up_ref[matrix] = grad_ref[start_up + matrix]


def add_kernel(offset, grad_ref, received_ref, total_ref):
    start = chunk_start(offset)
    for matrix in range(MATS_HERE):
        total_ref[matrix] = received_ref[matrix] + grad_ref[start + matrix]


def momentum_kernel(grad_ref, down_ref, up_ref, momentum_ref, *refs):
    out_ref = refs[-1]
    start = chunk_start(0)
    for matrix in range(MATS_HERE):
        own = grad_ref[start + matrix].astype(F32)
        summed = down_ref[matrix].astype(F32) + up_ref[matrix].astype(F32) + own
        out_ref[matrix] = (DECAY_RATE * momentum_ref[matrix] + summed).astype(out_ref.dtype)


def merge_kernel(pieces_ref, rows_ref):
    pieces = [pieces_ref[source].astype(F32) for source in range(PLANE_Y)]
    rows_ref[...] = jnp.concatenate(pieces, axis=0).astype(BF)


def split(value):
    high = value.astype(BF)
    return high, (value - high.astype(F32)).astype(BF)


def product(left, right, dims=(((1,), (0,)), ((), ()))):
    def one(a, b):
        return lax.dot_general(a, b, dims, preferred_element_type=F32)

    return one(left[0], right[0]) + (one(left[0], right[1]) + one(left[1], right[0]))


def gram_block(a, b):
    return lax.dot_general(a, b, NT, preferred_element_type=F32)


def own_gram_kernel(mine_ref, own_ref):
    mine = mine_ref[...]
    own_ref[...] = gram_block(mine, mine)


def orthogonal_kernel(own_ref, mine_ref, other_ref, out_ref, square_ref):
    mine = mine_ref[...]
    other = other_ref[...]
    cross = gram_block(mine, other)
    gram = jnp.concatenate(
        [
            jnp.concatenate([own_ref[...], cross], axis=1),
            jnp.concatenate([cross.T, gram_block(other, other)], axis=1),
        ],
        axis=0,
    )
    diagonal = lax.broadcasted_iota(jnp.int32, (ROWS, ROWS), 0) == lax.broadcasted_iota(jnp.int32, (ROWS, ROWS), 1)
    trace_sum = jnp.sum(jnp.where(diagonal, gram, 0.0))
    inverse = lax.rsqrt(jnp.full((1, 1), trace_sum + EPSILON, F32))
    scaled = gram * (inverse * inverse)
    first = jnp.where(diagonal, QUINTIC_FIRST, 0.0)
    square_form = scaled
    factor = None
    factor_scaled = split(scaled)
    for iteration in range(ITERS - 1):
        parts = split(square_form)
        polynomial = split(first + QUINTIC_SECOND * square_form + QUINTIC_THIRD * product(parts, parts))
        factor = polynomial if factor is None else split(product(polynomial, factor))
        factor_scaled = split(product(polynomial, factor_scaled))
        square_form = product(factor_scaled, factor, NT)
    start = pl.multiple_of(lax.div(lax.axis_index("shard"), PLANE_Y * CORES) * OWN_ROWS, OWN_ROWS)
    square_ref[...] = square_form
    own = square_ref[pl.ds(start, OWN_ROWS), :]
    column = lax.broadcasted_iota(jnp.int32, (OWN_ROWS, ROWS), 1)
    row = lax.broadcasted_iota(jnp.int32, (OWN_ROWS, ROWS), 0) + start
    polynomial = split(
        jnp.where(row == column, QUINTIC_FIRST, 0.0)
        + QUINTIC_SECOND * own
        + QUINTIC_THIRD * product(split(own), split(square_form))
    )
    coef = (product(polynomial, factor) * inverse).astype(BF)
    out_ref[...] = (
        jnp.dot(coef[:, :HALF], mine, preferred_element_type=F32)
        + jnp.dot(coef[:, HALF:], other, preferred_element_type=F32)
    ).astype(BF)


def update_kernel(returned_ref, mask_ref, update_ref):
    for matrix in range(MATS_HERE):
        update_ref[matrix] = returned_ref[matrix] * mask_ref[matrix]


def call(kernel, outs, *args, scratch=()):
    return pl.pallas_call(
        kernel,
        out_shape=outs,
        in_specs=[vmem() for _ in args],
        out_specs=jax.tree.map(lambda _: vmem(), outs),
        scratch_shapes=list(scratch),
        compiler_params=PARAMS,
    )(*args)


def shaped(shape, dtype):
    return jax.ShapeDtypeStruct(shape, dtype)


def local(grad_parts, momentum, mask_codes):
    grads = grad_parts[0]
    chunk = shaped(CHUNK, BF)

    def send(value, step):
        return lax.ppermute(value, "rep", [(i, (i + step) % REPS) for i in range(REPS)])

    def add(offset, received):
        return call(functools.partial(add_kernel, offset), chunk, grads, received)

    below = REPS // 2
    above = REPS - 1 - below
    down, up = call(functools.partial(first_kernel, -below, above), (chunk, chunk), grads)
    down, up = send(down, -1), send(up, 1)
    for step in range(1, below):
        down = send(add(step - below, down), -1)
        if step < above:
            up = send(add(above - step, up), 1)
        if step == 2:
            up, codes = lax.optimization_barrier((up, mask_codes))
            mask = call(mask_kernel, chunk, codes)
        if step == 4:
            up, mask = lax.optimization_barrier((up, mask))
    outgoing = call(momentum_kernel, chunk, grads, down, up, momentum)
    pieces = lax.all_to_all(outgoing, "shard", split_axis=0, concat_axis=0, tiled=True, axis_index_groups=GROUPS_Y)
    pieces = call(merge_kernel, shaped((OWN_ROWS, COLS), BF), pieces)
    mine = lax.all_gather(pieces, "shard", axis=0, tiled=True, axis_index_groups=GROUPS_X)
    other = lax.ppermute(mine, "shard", OTHER_CORE)
    own_gram = call(own_gram_kernel, shaped((HALF, HALF), F32), mine)
    momentum_next = call(momentum_kernel, shaped(CHUNK, F32), grads, down, up, momentum, own_gram)
    other, own_gram, momentum_next = lax.optimization_barrier((other, own_gram, momentum_next))
    orthogonal = call(
        orthogonal_kernel,
        shaped((OWN_ROWS, COLS), BF),
        own_gram,
        mine,
        other,
        scratch=[pltpu.VMEM((ROWS, ROWS), F32)],
    )
    returned = lax.all_to_all(
        orthogonal.reshape(CHUNK), "shard", split_axis=0, concat_axis=0, tiled=True, axis_index_groups=GROUPS_Y
    )
    update = call(update_kernel, chunk, returned, mask)
    return (momentum_next, update)


def solution(mesh):
    in_specs = (P("rep", None, "shard", None), P("rep", "shard", None), P("rep", "shard", None))
    out_specs = (P("rep", "shard", None), P("rep", "shard", None))
    return jax.shard_map(local, mesh=mesh, in_specs=in_specs, out_specs=out_specs, check_vma=False)
```

```python
import functools

import jax
import jax.numpy as jnp
from jax import lax
from jax.experimental import pallas as pl
from jax.experimental.pallas import tpu as pltpu
from jax.sharding import PartitionSpec as P

ITERS = 5
DECAY_RATE = 0.95
EPSILON = 1e-07
QUINTIC_FIRST = 3.4445
QUINTIC_SECOND = -4.775
QUINTIC_THIRD = 2.0315
UPDATE_SCALE = 64.0

REPS = 12
MATS_HERE = 8
PIECE_ROWS = 4
COLS = 3584
ROWS = 256
HALF = ROWS // 2
PLANE_X = 4
PLANE_Y = 8
CORES = 2
SHARDS = PLANE_X * PLANE_Y * CORES
OWN_ROWS = PLANE_Y * PIECE_ROWS
BF = jnp.bfloat16
F32 = jnp.float32
CHUNK = (MATS_HERE, PIECE_ROWS, COLS)
PARAMS = pltpu.CompilerParams(vmem_limit_bytes=8 * 1024 * 1024)
NT = (((1,), (1,)), ((), ()))


def shard_index(x, y, core):
    return (x * PLANE_Y + y) * CORES + core


GROUPS_Y = [[shard_index(x, y, c) for y in range(PLANE_Y)] for x in range(PLANE_X) for c in range(CORES)]
GROUPS_X = [[shard_index(x, y, c) for x in range(PLANE_X)] for y in range(PLANE_Y) for c in range(CORES)]
OTHER_CORE = [(i, i ^ 1) for i in range(SHARDS)]


def vmem():
    return pl.BlockSpec(memory_space=pltpu.VMEM)


def mask_kernel(codes_ref, mask_ref):
    group = lax.broadcasted_iota(jnp.int32, (128, 512), 0)
    column = lax.broadcasted_iota(jnp.int32, (128, 512), 1)
    spread = jnp.where((column >> 2) == group, 1.0, 0.0).astype(BF)
    place = lax.broadcasted_iota(jnp.int32, (MATS_HERE * PIECE_ROWS, 512), 1) & 3
    for block in range(7):
        here = slice(block * 128, (block + 1) * 128)
        code = jnp.concatenate([codes_ref[matrix, :, here] for matrix in range(MATS_HERE)], axis=0)
        pair = jnp.where(code == 0, 3, jnp.where(code == 1, 5, jnp.where(code == 2, 9, 0)))
        pair = jnp.where(code == 3, 6, jnp.where(code == 4, 10, jnp.where(code == 5, 12, pair)))
        wide = jnp.dot(pair.astype(F32).astype(BF), spread, preferred_element_type=F32).astype(jnp.int32)
        kept = ((wide >> place) & 1).astype(F32) * UPDATE_SCALE
        for matrix in range(MATS_HERE):
            rows = kept[matrix * PIECE_ROWS : (matrix + 1) * PIECE_ROWS]
            mask_ref[matrix, :, block * 512 : (block + 1) * 512] = rows.astype(BF)


def chunk_start(offset):
    place = lax.rem(lax.axis_index("rep") + offset % REPS, REPS)
    return place * MATS_HERE


def first_kernel(below, above, grad_ref, down_ref, up_ref):
    start_down, start_up = chunk_start(below), chunk_start(above)
    for matrix in range(MATS_HERE):
        down_ref[matrix] = grad_ref[start_down + matrix]
        up_ref[matrix] = grad_ref[start_up + matrix]


def add_kernel(offset, grad_ref, received_ref, total_ref):
    start = chunk_start(offset)
    for matrix in range(MATS_HERE):
        total_ref[matrix] = received_ref[matrix] + grad_ref[start + matrix]


def momentum_kernel(grad_ref, down_ref, up_ref, momentum_ref, *refs):
    out_ref = refs[-1]
    start = chunk_start(0)
    for matrix in range(MATS_HERE):
        own = grad_ref[start + matrix].astype(F32)
        summed = down_ref[matrix].astype(F32) + up_ref[matrix].astype(F32) + own
        out_ref[matrix] = (DECAY_RATE * momentum_ref[matrix] + summed).astype(out_ref.dtype)


def merge_kernel(pieces_ref, rows_ref):
    pieces = [pieces_ref[source].astype(F32) for source in range(PLANE_Y)]
    rows_ref[...] = jnp.concatenate(pieces, axis=0).astype(BF)


def split(value):
    high = value.astype(BF)
    return high, (value - high.astype(F32)).astype(BF)


def product(left, right, dims=(((1,), (0,)), ((), ()))):
    def one(a, b):
        return lax.dot_general(a, b, dims, preferred_element_type=F32)

    return one(left[0], right[0]) + (one(left[0], right[1]) + one(left[1], right[0]))


def gram_block(a, b):
    return lax.dot_general(a, b, NT, preferred_element_type=F32)


def own_gram_kernel(mine_ref, own_ref):
    mine = mine_ref[...]
    own_ref[...] = gram_block(mine, mine)


def orthogonal_kernel(own_ref, mine_ref, other_ref, out_ref, square_ref):
    mine = mine_ref[...]
    other = other_ref[...]
    beside = gram_block(jnp.concatenate([mine, other], axis=0), other)
    cross = beside[:HALF]
    gram = jnp.concatenate(
        [
            jnp.concatenate([own_ref[...], cross], axis=1),
            jnp.concatenate([cross.T, beside[HALF:]], axis=1),
        ],
        axis=0,
    )
    diagonal = lax.broadcasted_iota(jnp.int32, (ROWS, ROWS), 0) == lax.broadcasted_iota(jnp.int32, (ROWS, ROWS), 1)
    trace_sum = jnp.sum(jnp.where(diagonal, gram, 0.0))
    inverse = lax.rsqrt(jnp.full((1, 1), trace_sum + EPSILON, F32))
    scaled = gram * (inverse * inverse)
    first = jnp.where(diagonal, QUINTIC_FIRST, 0.0)
    square_form = scaled
    factor = None
    factor_scaled = split(scaled)
    for iteration in range(ITERS - 1):
        parts = split(square_form)
        polynomial = split(first + QUINTIC_SECOND * square_form + QUINTIC_THIRD * product(parts, parts))
        factor = polynomial if factor is None else split(product(polynomial, factor))
        factor_scaled = split(product(polynomial, factor_scaled))
        square_form = product(factor_scaled, factor, NT)
    start = pl.multiple_of(lax.div(lax.axis_index("shard"), PLANE_Y * CORES) * OWN_ROWS, OWN_ROWS)
    square_ref[...] = square_form
    own = square_ref[pl.ds(start, OWN_ROWS), :]
    column = lax.broadcasted_iota(jnp.int32, (OWN_ROWS, ROWS), 1)
    row = lax.broadcasted_iota(jnp.int32, (OWN_ROWS, ROWS), 0) + start
    polynomial = split(
        jnp.where(row == column, QUINTIC_FIRST, 0.0)
        + QUINTIC_SECOND * own
        + QUINTIC_THIRD * product(split(own), split(square_form))
    )
    coef = (product(polynomial, factor) * inverse).astype(BF)
    own_rows = jnp.dot(coef[:, :HALF], mine, preferred_element_type=F32) + jnp.dot(
        coef[:, HALF:], other, preferred_element_type=F32
    )
    for target in range(PLANE_Y):
        out_ref[target] = own_rows[target * PIECE_ROWS : (target + 1) * PIECE_ROWS].astype(BF)


def update_kernel(returned_ref, mask_ref, update_ref):
    for matrix in range(MATS_HERE):
        update_ref[matrix] = returned_ref[matrix] * mask_ref[matrix]


def call(kernel, outs, *args, scratch=()):
    return pl.pallas_call(
        kernel,
        out_shape=outs,
        in_specs=[vmem() for _ in args],
        out_specs=jax.tree.map(lambda _: vmem(), outs),
        scratch_shapes=list(scratch),
        compiler_params=PARAMS,
    )(*args)


def shaped(shape, dtype):
    return jax.ShapeDtypeStruct(shape, dtype)


def local(grad_parts, momentum, mask_codes):
    grads = grad_parts[0]
    chunk = shaped(CHUNK, BF)

    def send(value, step):
        return lax.ppermute(value, "rep", [(i, (i + step) % REPS) for i in range(REPS)])

    def add(offset, received):
        return call(functools.partial(add_kernel, offset), chunk, grads, received)

    below = REPS // 2
    above = REPS - 1 - below
    down, up = call(functools.partial(first_kernel, -below, above), (chunk, chunk), grads)
    down, up = send(down, -1), send(up, 1)
    for step in range(1, below):
        down = send(add(step - below, down), -1)
        if step < above:
            up = send(add(above - step, up), 1)
        if step == 2:
            up, codes = lax.optimization_barrier((up, mask_codes))
            mask = call(mask_kernel, chunk, codes)
        if step == 4:
            up, mask = lax.optimization_barrier((up, mask))
    outgoing = call(momentum_kernel, chunk, grads, down, up, momentum)
    pieces = lax.all_to_all(outgoing, "shard", split_axis=0, concat_axis=0, tiled=True, axis_index_groups=GROUPS_Y)
    pieces = call(merge_kernel, shaped((OWN_ROWS, COLS), BF), pieces)
    mine = lax.all_gather(pieces, "shard", axis=0, tiled=True, axis_index_groups=GROUPS_X)
    other = lax.ppermute(mine, "shard", OTHER_CORE)
    own_gram = call(own_gram_kernel, shaped((HALF, HALF), F32), mine)
    momentum_next = call(momentum_kernel, shaped(CHUNK, F32), grads, down, up, momentum, own_gram)
    other, own_gram, momentum_next = lax.optimization_barrier((other, own_gram, momentum_next))
    orthogonal = call(
        orthogonal_kernel,
        chunk,
        own_gram,
        mine,
        other,
        scratch=[pltpu.VMEM((ROWS, ROWS), F32)],
    )
    returned = lax.all_to_all(
        orthogonal, "shard", split_axis=0, concat_axis=0, tiled=True, axis_index_groups=GROUPS_Y
    )
    update = call(update_kernel, chunk, returned, mask)
    return (momentum_next, update)


def solution(mesh):
    in_specs = (P("rep", None, "shard", None), P("rep", "shard", None), P("rep", "shard", None))
    out_specs = (P("rep", "shard", None), P("rep", "shard", None))
    return jax.shard_map(local, mesh=mesh, in_specs=in_specs, out_specs=out_specs, check_vma=False)
```

```python
import functools

import jax
import jax.numpy as jnp
from jax import lax
from jax.experimental import pallas as pl
from jax.experimental.pallas import tpu as pltpu
from jax.sharding import PartitionSpec as P

ITERS = 5
DECAY_RATE = 0.95
EPSILON = 1e-07
QUINTIC_FIRST = 3.4445
QUINTIC_SECOND = -4.775
QUINTIC_THIRD = 2.0315
UPDATE_SCALE = 64.0

REPS = 12
MATS_HERE = 8
PIECE_ROWS = 4
COLS = 3584
ROWS = 256
HALF = ROWS // 2
PLANE_X = 4
PLANE_Y = 8
CORES = 2
SHARDS = PLANE_X * PLANE_Y * CORES
OWN_ROWS = PLANE_Y * PIECE_ROWS
BF = jnp.bfloat16
F32 = jnp.float32
CHUNK = (MATS_HERE, PIECE_ROWS, COLS)
PARAMS = pltpu.CompilerParams(vmem_limit_bytes=8 * 1024 * 1024)
NT = (((1,), (1,)), ((), ()))


def shard_index(x, y, core):
    return (x * PLANE_Y + y) * CORES + core


GROUPS_Y = [[shard_index(x, y, c) for y in range(PLANE_Y)] for x in range(PLANE_X) for c in range(CORES)]
GROUPS_X = [[shard_index(x, y, c) for x in range(PLANE_X)] for y in range(PLANE_Y) for c in range(CORES)]
OTHER_CORE = [(i, i ^ 1) for i in range(SHARDS)]


def vmem():
    return pl.BlockSpec(memory_space=pltpu.VMEM)


def mask_kernel(codes_ref, mask_ref):
    group = lax.broadcasted_iota(jnp.int32, (128, 512), 0)
    column = lax.broadcasted_iota(jnp.int32, (128, 512), 1)
    spread = jnp.where((column >> 2) == group, 1.0, 0.0).astype(BF)
    place = lax.broadcasted_iota(jnp.int32, (MATS_HERE * PIECE_ROWS, 512), 1) & 3
    for block in range(7):
        here = slice(block * 128, (block + 1) * 128)
        code = jnp.concatenate([codes_ref[matrix, :, here] for matrix in range(MATS_HERE)], axis=0)
        pair = jnp.where(code == 0, 3, jnp.where(code == 1, 5, jnp.where(code == 2, 9, 0)))
        pair = jnp.where(code == 3, 6, jnp.where(code == 4, 10, jnp.where(code == 5, 12, pair)))
        wide = jnp.dot(pair.astype(F32).astype(BF), spread, preferred_element_type=F32).astype(jnp.int32)
        kept = ((wide >> place) & 1).astype(F32) * UPDATE_SCALE
        for matrix in range(MATS_HERE):
            rows = kept[matrix * PIECE_ROWS : (matrix + 1) * PIECE_ROWS]
            mask_ref[matrix, :, block * 512 : (block + 1) * 512] = rows.astype(BF)


def chunk_start(offset):
    place = lax.rem(lax.axis_index("rep") + offset % REPS, REPS)
    return place * MATS_HERE


def first_kernel(below, above, grad_ref, down_ref, up_ref):
    start_down, start_up = chunk_start(below), chunk_start(above)
    for matrix in range(MATS_HERE):
        down_ref[matrix] = grad_ref[start_down + matrix]
        up_ref[matrix] = grad_ref[start_up + matrix]


def add_kernel(offset, grad_ref, received_ref, total_ref):
    start = chunk_start(offset)
    for matrix in range(MATS_HERE):
        total_ref[matrix] = received_ref[matrix] + grad_ref[start + matrix]


def momentum_kernel(grad_ref, down_ref, up_ref, momentum_ref, *refs):
    out_ref = refs[-1]
    start = chunk_start(0)
    for matrix in range(MATS_HERE):
        own = grad_ref[start + matrix].astype(F32)
        summed = down_ref[matrix].astype(F32) + up_ref[matrix].astype(F32) + own
        out_ref[matrix] = (DECAY_RATE * momentum_ref[matrix] + summed).astype(out_ref.dtype)


def merge_kernel(pieces_ref, rows_ref):
    pieces = [pieces_ref[source].astype(F32) for source in range(PLANE_Y)]
    rows_ref[...] = jnp.concatenate(pieces, axis=0).astype(BF)


def split(value):
    high = value.astype(BF)
    return high, (value - high.astype(F32)).astype(BF)


def product(left, right, dims=(((1,), (0,)), ((), ()))):
    def one(a, b):
        return lax.dot_general(a, b, dims, preferred_element_type=F32)

    return one(left[0], right[0]) + (one(left[0], right[1]) + one(left[1], right[0]))


def gram_block(a, b):
    return lax.dot_general(a, b, NT, preferred_element_type=F32)


def own_gram_kernel(mine_ref, own_ref):
    mine = mine_ref[...]
    own_ref[...] = gram_block(mine, mine)


def orthogonal_kernel(own_ref, mine_ref, other_ref, out_ref, square_ref):
    mine = mine_ref[...]
    other = other_ref[...]
    beside = gram_block(jnp.concatenate([mine, other], axis=0), other)
    cross = beside[:HALF]
    gram = jnp.concatenate(
        [
            jnp.concatenate([own_ref[...], cross], axis=1),
            jnp.concatenate([cross.T, beside[HALF:]], axis=1),
        ],
        axis=0,
    )
    diagonal = lax.broadcasted_iota(jnp.int32, (ROWS, ROWS), 0) == lax.broadcasted_iota(jnp.int32, (ROWS, ROWS), 1)
    trace_sum = jnp.sum(jnp.where(diagonal, gram, 0.0))
    inverse = lax.rsqrt(jnp.full((1, 1), trace_sum + EPSILON, F32))
    scaled = gram * (inverse * inverse)
    first = jnp.where(diagonal, QUINTIC_FIRST, 0.0)
    square_form = scaled
    factor = None
    factor_scaled = split(scaled)
    for iteration in range(ITERS - 1):
        parts = split(square_form)
        polynomial = split(first + QUINTIC_SECOND * square_form + QUINTIC_THIRD * product(parts, parts))
        factor = polynomial if factor is None else split(product(polynomial, factor))
        factor_scaled = split(product(polynomial, factor_scaled))
        square_form = product(factor_scaled, factor, NT)
    start = pl.multiple_of(lax.div(lax.axis_index("shard"), PLANE_Y * CORES) * OWN_ROWS, OWN_ROWS)
    square_ref[...] = square_form
    own = square_ref[pl.ds(start, OWN_ROWS), :]
    column = lax.broadcasted_iota(jnp.int32, (OWN_ROWS, ROWS), 1)
    row = lax.broadcasted_iota(jnp.int32, (OWN_ROWS, ROWS), 0) + start
    polynomial = split(
        jnp.where(row == column, QUINTIC_FIRST, 0.0)
        + QUINTIC_SECOND * own
        + QUINTIC_THIRD * product(split(own), split(square_form))
    )
    coef = (product(polynomial, factor) * inverse).astype(BF)
    out_ref[...] = (
        jnp.dot(coef[:, :HALF], mine, preferred_element_type=F32)
        + jnp.dot(coef[:, HALF:], other, preferred_element_type=F32)
    ).astype(BF)


def update_kernel(returned_ref, mask_ref, update_ref):
    for matrix in range(MATS_HERE):
        update_ref[matrix] = returned_ref[matrix] * mask_ref[matrix]


def call(kernel, outs, *args, scratch=()):
    return pl.pallas_call(
        kernel,
        out_shape=outs,
        in_specs=[vmem() for _ in args],
        out_specs=jax.tree.map(lambda _: vmem(), outs),
        scratch_shapes=list(scratch),
        compiler_params=PARAMS,
    )(*args)


def shaped(shape, dtype):
    return jax.ShapeDtypeStruct(shape, dtype)


def local(grad_parts, momentum, mask_codes):
    grads = grad_parts[0]
    chunk = shaped(CHUNK, BF)

    def send(value, step):
        return lax.ppermute(value, "rep", [(i, (i + step) % REPS) for i in range(REPS)])

    def add(offset, received):
        return call(functools.partial(add_kernel, offset), chunk, grads, received)

    below = REPS // 2
    above = REPS - 1 - below
    down, up = call(functools.partial(first_kernel, -below, above), (chunk, chunk), grads)
    down, up = send(down, -1), send(up, 1)
    for step in range(1, below):
        down = send(add(step - below, down), -1)
        if step < above:
            up = send(add(above - step, up), 1)
        if step == 2:
            up, codes = lax.optimization_barrier((up, mask_codes))
            mask = call(mask_kernel, chunk, codes)
        if step == 4:
            up, mask = lax.optimization_barrier((up, mask))
    outgoing = call(momentum_kernel, chunk, grads, down, up, momentum)
    pieces = lax.all_to_all(outgoing, "shard", split_axis=0, concat_axis=0, tiled=True, axis_index_groups=GROUPS_Y)
    pieces = call(merge_kernel, shaped((OWN_ROWS, COLS), BF), pieces)
    mine = lax.all_gather(pieces, "shard", axis=0, tiled=True, axis_index_groups=GROUPS_X)
    other = lax.ppermute(mine, "shard", OTHER_CORE)
    own_gram = call(own_gram_kernel, shaped((HALF, HALF), F32), mine)
    momentum_next = call(momentum_kernel, shaped(CHUNK, F32), grads, down, up, momentum, own_gram)
    other, own_gram, momentum_next = lax.optimization_barrier((other, own_gram, momentum_next))
    orthogonal = call(
        orthogonal_kernel,
        shaped((OWN_ROWS, COLS), BF),
        own_gram,
        mine,
        other,
        scratch=[pltpu.VMEM((ROWS, ROWS), F32)],
    )
    returned = lax.all_to_all(
        orthogonal.reshape(CHUNK), "shard", split_axis=0, concat_axis=0, tiled=True, axis_index_groups=GROUPS_Y
    )
    update = call(update_kernel, chunk, returned, mask)
    return (momentum_next, update)


def solution(mesh):
    in_specs = (P("rep", None, "shard", None), P("rep", "shard", None), P("rep", "shard", None))
    out_specs = (P("rep", "shard", None), P("rep", "shard", None))
    return jax.shard_map(local, mesh=mesh, in_specs=in_specs, out_specs=out_specs, check_vma=False)
```
